32 devices in a mesh: slab: 4 (over z), cross: 8 (over y, x, core).
Axes of the slice: x: 2, y: 2, z: 4, core: 2. Of those that a mesh axis runs over, the one named last changes fastest.
Arguments:
- thickness: int32 [4], P('slab'), may hold values from 1 to 4, as said below
- layer_sources: bfloat16 [16, 128, 32768], P('slab', None, 'cross'), may hold values from -6 to 6
- green_down: bfloat16 [4, 1536, 128, 128], P('slab', 'cross'), may hold values from -0.1875 to 0.1875
- column_down: int32 [4, 1536], P('slab', 'cross'), may hold values from 0 to 255, as said below
- green_up: bfloat16 [4, 1536, 128, 128], P('slab', 'cross'), may hold values from -0.1875 to 0.1875
- column_up: int32 [4, 1536], P('slab', 'cross'), may hold values from 0 to 255, as said below
Outputs:
- down_traces: bfloat16 [4, 128, 32768], P('slab', None, 'cross')
- up_traces: bfloat16 [4, 128, 32768], P('slab', None, 'cross')
The draws below stay inside these ranges and needn't reach their ends.
Inputs may be any that keep to these rules, and one draw needn't show every extreme that they name: `thickness`: each slab has 1 to 4 layers; some slab has exactly 4 and another exactly 1. `column_down`: the 6 columns of block row i are distinct, each equals (i + o) modulo 256 for some o with -4 <= o <= 4, and they include (i + 4) modulo 256. `column_up`: as for column_down.
All inputs are finite; a program needn't handle non-finite values.
Results may differ from the reference program's by a relative error of at most 0.015.
Values may be sent and summed in bfloat16 or wider, within the bound.
No kernel may reach another device: no remote copies, remote signals or barrier semaphores. Data moves between devices by JAX's collectives and lax.ppermute only.
A program may use at most 64 MiB of HBM per device.

```python
import jax
import jax.numpy as jnp

TR = 32768
BS = 128
KB = 6
HB = 4
TMAX = 4
SRC = 128
NB = 256
LAYERS = 16
N_SLAB = 4


def draw_thickness(key, part):
    first = jax.random.fold_in(key, 11)
    second = jax.random.fold_in(key, 12)
    third = jax.random.fold_in(key, 13)
    values = jax.random.randint(first, (N_SLAB,), 1, TMAX + 1)
    where_max = jax.random.randint(second, (), 0, N_SLAB)
    step_min = jax.random.randint(third, (), 1, N_SLAB)
    where_min = (where_max + step_min) % N_SLAB
    slots = jnp.arange(N_SLAB)
    values = jnp.where(slots == where_min, 1, values)
    return jnp.where(slots == where_max, TMAX, values).astype(jnp.int32)


def block_columns(key):
    keys = jax.random.split(key, N_SLAB * NB)
    inner = jax.vmap(lambda one: jax.random.permutation(one, 2 * HB)[:KB - 1])(keys)
    inner = inner.astype(jnp.int32) - HB
    ends = jnp.full((N_SLAB * NB, 1), HB, jnp.int32)
    offsets = jnp.concatenate([ends, inner], axis=1)
    offsets = offsets.reshape(N_SLAB, NB, KB)
    rows = jnp.arange(NB)[None, :, None]
    return ((rows + offsets) % NB).reshape(N_SLAB, NB * KB).astype(jnp.int32)


def draw_column_down(key, part):
    return block_columns(jax.random.fold_in(key, 21))


def draw_column_up(key, part):
    return block_columns(jax.random.fold_in(key, 22))


def level_of(own_key, dims, pieces, smallest, largest):
    loudness = 1.0
    for position, parts in pieces:
        steps = jax.random.uniform(jax.random.fold_in(jax.random.fold_in(own_key, 6), position), (parts,), jnp.float32, smallest / len(pieces), largest / len(pieces))
        loudness = loudness * jnp.repeat(jnp.exp(steps), dims[position] // parts).reshape((-1,) + (1,) * (len(dims) - 1 - position))
    return loudness


def noise(rng, dims, width, bound, shards=(), held_as=jnp.bfloat16):
    result = jax.random.normal(rng, dims, jnp.float32) * width
    if len(shards) > 0:
        result = level_of(rng, dims, shards, -0.22, 0.18) * result
    return jnp.clip(result, min=-bound, max=bound).astype(held_as)


def setup_inputs(seed: int = 0) -> dict:
    splits = jax.random.split(jax.random.key(seed), 7)
    thickness = draw_thickness(jax.random.fold_in(splits[6], 71), 0)
    layer_sources = noise(splits[1], (LAYERS, SRC, TR), 1.0, 6.0, ((0, 4), (2, 8)))
    green_down = noise(splits[2], (N_SLAB, NB * KB, BS, BS), (KB * BS * 7 // 5) ** -0.5, 0.1875, ((0, 4), (1, 8)))
    column_down = draw_column_down(jax.random.fold_in(splits[6], 71), 0)
    green_up = noise(splits[4], (N_SLAB, NB * KB, BS, BS), (KB * BS * 7 // 5) ** -0.5, 0.1875, ((0, 4), (1, 8)))
    column_up = draw_column_up(jax.random.fold_in(splits[6], 71), 0)
    return dict(thickness=thickness, layer_sources=layer_sources, green_down=green_down, column_down=column_down, green_up=green_up, column_up=column_up)


def apply_green(trace, blocks, columns):
    rows = trace.shape[0]
    nblk = trace.shape[1] // blocks.shape[-1]
    bsize = blocks.shape[-1]
    tiles = trace.astype(jnp.float32).reshape(rows, nblk, bsize)
    picked = jnp.take(tiles, columns, axis=1)
    prod = jnp.einsum("snb,nab->sna", picked, blocks.astype(jnp.float32))
    kcount = blocks.shape[0] // nblk
    return prod.reshape(rows, nblk, kcount, bsize).sum(axis=2).reshape(rows, nblk * bsize)


def slab_source(layer_sources, thickness, slab_id):
    depth = layer_sources.shape[0] // thickness.shape[0]
    layers = jax.lax.dynamic_slice_in_dim(layer_sources, slab_id * depth, depth, 0).astype(jnp.float32)
    keep = (jnp.arange(depth) < thickness[slab_id]).astype(jnp.float32)
    return jnp.sum(layers * keep[:, None, None], axis=0)


def reference(thickness, layer_sources, green_down, column_down, green_up, column_up):
    slabs = thickness.shape[0]
    downs = []
    previous = None
    for slab_id in range(slabs):
        value = slab_source(layer_sources, thickness, slab_id)
        if previous is not None:
            value = value + apply_green(previous, green_down[slab_id], column_down[slab_id])
        previous = value.astype(jnp.bfloat16)
        downs.append(previous)
    ups = [None] * slabs
    previous = None
    for slab_id in range(slabs - 1, -1, -1):
        value = slab_source(layer_sources, thickness, slab_id)
        if previous is not None:
            value = value + apply_green(previous, green_up[slab_id], column_up[slab_id])
        previous = value.astype(jnp.bfloat16)
        ups[slab_id] = previous
    return jnp.stack(downs), jnp.stack(ups)
```

```python
import functools

import jax
import jax.numpy as jnp
from jax import lax
from jax.experimental import pallas as pl
from jax.experimental.pallas import tpu as pltpu
from jax.sharding import PartitionSpec as P

HB = 4
CHUNKS = 2
VMEM = pl.BlockSpec(memory_space=pltpu.VMEM)
SMEM = pl.BlockSpec(memory_space=pltpu.SMEM)
ANY = pl.BlockSpec(memory_space=pl.ANY)
HBM = pl.BlockSpec(memory_space=pltpu.HBM)


def params(mib):
    return pltpu.CompilerParams(vmem_limit_bytes=mib << 20)


def source_kernel(row0, halo, thick_ref, layers_ref, total_ref, *rest):
    *outs, buf, sems = rest
    depth, rows, width = buf.shape
    thick = thick_ref[0]

    def copy(k):
        return pltpu.make_async_copy(
            layers_ref.at[k, pl.ds(row0, rows), :], buf.at[k], sems.at[k]
        )

    for k in range(depth):
        pl.when(k < thick)(copy(k).start)
    total_ref[...] = jnp.zeros_like(total_ref)
    for k in range(depth):

        @pl.when(k < thick)
        def _():
            copy(k).wait()
            total_ref[...] += buf[k].astype(jnp.float32)

    put(outs, total_ref[...].astype(jnp.bfloat16), 0, halo)


def put(outs, value, start, halo):
    if len(outs) == 1:
        outs[0][:, start : start + value.shape[1]] = value
        return
    edges, mid = outs
    width = edges.shape[1] + mid.shape[1]
    stop = start + value.shape[1]
    for lo, hi, ref, shift in (
        (0, halo, edges, 0),
        (halo, width - halo, mid, -halo),
        (width - halo, width, edges, 2 * halo - width),
    ):
        a, b = max(lo, start), min(hi, stop)
        if a < b:
            ref[:, a + shift : b + shift] = value[:, a - start : b - start]


def product_kernel(halo, parts, mode_ref, cols_ref, left_ref, right_ref, *rest):
    ins, (down_ref, up_ref, total_ref), outs, ext = (
        rest[:parts],
        rest[parts : parts + 3],
        rest[parts + 3 : -1],
        rest[-1],
    )
    width = total_ref.shape[1]
    bsize = down_ref.shape[-1]
    per_dev = width // bsize
    kcount = down_ref.shape[1] // per_dev

    def apply(green_ref):
        ext[:, :halo] = left_ref[...]
        ext[:, halo + width :] = right_ref[...]
        if parts == 1:
            ext[:, halo : halo + width] = ins[0][...]
        else:
            ext[:, halo : 2 * halo] = ins[0][:, :halo]
            ext[:, 2 * halo : width] = ins[1][...]
            ext[:, width : width + halo] = ins[0][:, halo:]
        for i in range(per_dev):
            picked, blocks = [], []
            for k in range(kcount):
                at = pl.multiple_of(cols_ref[0, i * kcount + k] * bsize, bsize)
                picked.append(ext[:, pl.ds(at, bsize)])
                blocks.append(green_ref[0, i * kcount + k])
            value = lax.dot_general(
                jnp.concatenate(picked, 1),
                jnp.concatenate(blocks, 1),
                (((1,), (1,)), ((), ())),
                preferred_element_type=jnp.float32,
            )
            value = value + total_ref[:, i * bsize : (i + 1) * bsize]
            put(outs, value.astype(jnp.bfloat16), i * bsize, halo)

    pl.when(mode_ref[0] == 1)(lambda: apply(down_ref))
    pl.when(mode_ref[0] == 2)(lambda: apply(up_ref))


def store_kernel(halo, hops, chunks, parts, slab_ref, *rest):
    ins, (down_ref, up_ref), sems = rest[:-3], rest[-3:-1], rest[-1]
    rows = ins[0].shape[0]
    width = down_ref.shape[2]

    def copies(h, out_ref, which):
        made = []
        for j in range(chunks):
            at = (h * chunks + j) * parts
            span = pl.ds(j * rows, rows)
            if parts == 1:
                pieces = [(ins[at], 0, width, 0)]
            else:
                pieces = [
                    (ins[at], 0, halo, 0),
                    (ins[at + 1], 0, width - 2 * halo, halo),
                    (ins[at], halo, halo, width - halo),
                ]
            for src, a, size, b in pieces:
                made.append(
                    pltpu.make_async_copy(
                        src.at[:, pl.ds(a, size)],
                        out_ref.at[0, span, pl.ds(b, size)],
                        sems.at[which, len(made)],
                    )
                )
        return made

    plan = []
    for h in range(hops):
        plan.append((h, down_ref, 0, slab_ref[0] == h))
        plan.append((h, up_ref, 1, slab_ref[0] == hops - 1 - h))
    for h, ref, which, chosen in plan:

        @pl.when(chosen)
        def _():
            for copy in copies(h, ref, which):
                copy.start()

    for h, ref, which, chosen in plan:

        @pl.when(chosen)
        def _():
            for copy in copies(h, ref, which):
                copy.wait()


def shards(thickness, layer_sources, green_down, column_down, green_up, column_up):
    slabs = lax.axis_size("slab")
    cross = lax.axis_size("cross")
    slab_id = lax.axis_index("slab")
    lateral = lax.axis_index("cross")
    depth, sources, width = layer_sources.shape
    bsize = green_down.shape[-1]
    per_dev = width // bsize
    total_blocks = per_dev * cross
    nblocks = green_down.shape[1]
    halo = HB * bsize
    rows = sources // CHUNKS
    split = per_dev > 2 * HB
    parts = 2 if split else 1
    low = slab_id < slabs // 2
    bf16 = lambda cols: jax.ShapeDtypeStruct((rows, cols), jnp.bfloat16)
    pieces = [bf16(2 * halo), bf16(width - 2 * halo)] if split else [bf16(width)]

    def local(first):
        cols = jnp.where(first, column_down, column_up)
        return (cols - lateral * per_dev + HB) % total_blocks

    def source(j):
        total, *out = pl.pallas_call(
            functools.partial(source_kernel, j * rows, halo),
            out_shape=[jax.ShapeDtypeStruct((rows, width), jnp.float32), *pieces],
            in_specs=[SMEM, HBM],
            out_specs=[VMEM] * (1 + parts),
            scratch_shapes=[
                pltpu.VMEM((depth, rows, width), jnp.bfloat16),
                pltpu.SemaphoreType.DMA((depth,)),
            ],
            compiler_params=params(16),
            name="source",
        )(thickness, layer_sources)
        return total, out

    def product(h, cols, left, right, got, total):
        mode = jnp.where(slab_id == h, 1, jnp.where(slab_id == slabs - 1 - h, 2, 0))
        return pl.pallas_call(
            functools.partial(product_kernel, halo, parts),
            out_shape=pieces,
            in_specs=[SMEM, SMEM] + [VMEM] * (5 + parts),
            out_specs=[VMEM] * parts,
            scratch_shapes=[pltpu.VMEM((rows, width + 2 * halo), jnp.bfloat16)],
            compiler_params=params(24),
            cost_estimate=pl.CostEstimate(
                flops=2 * rows * nblocks * bsize * bsize,
                bytes_accessed=nblocks * bsize * bsize * 2,
                transcendentals=0,
            ),
            name="product",
        )(mode.reshape(1), cols, left, right, *got, green_down, green_up, total)

    def hop(x, h):
        route = []
        for a, b in ((h - 1, h), (slabs - h, slabs - 1 - h)):
            route += [(a * cross + c, b * cross + c) for c in range(cross)]
        return lax.ppermute(x, ("slab", "cross"), route)

    def sideways(x, step):
        return lax.ppermute(x, "cross", [(c, (c + step) % cross) for c in range(cross)])

    totals, made = [], {}
    for j in range(CHUNKS):
        total, out = source(j)
        totals.append(total)
        made[0, j] = out
    cols = [local(low), local(jnp.logical_not(low))]
    order = sorted(
        ((h, j) for h in range(1, slabs) for j in range(CHUNKS)),
        key=lambda hj: (hj[0] + hj[1], hj[0]),
    )
    for h, j in order:
        got = [hop(x, h) for x in made[h - 1, j]]
        right = sideways(got[0][:, :halo], -1)
        left = sideways(got[0][:, got[0].shape[1] - halo :], 1)
        late = 0 if h < slabs // 2 else 1
        made[h, j] = product(h, cols[late], left, right, got, totals[j])

    flat = [x for h in range(slabs) for j in range(CHUNKS) for x in made[h, j]]
    return pl.pallas_call(
        functools.partial(store_kernel, halo, slabs, CHUNKS, parts),
        out_shape=[jax.ShapeDtypeStruct((1, sources, width), jnp.bfloat16)] * 2,
        in_specs=[SMEM] + [VMEM] * len(flat),
        out_specs=[ANY, ANY],
        scratch_shapes=[pltpu.SemaphoreType.DMA((2, CHUNKS * (3 if split else 1)))],
        compiler_params=params(16),
        name="store",
    )(slab_id.astype(jnp.int32).reshape(1), *flat)


def solution(mesh):
    return jax.shard_map(
        shards,
        mesh=mesh,
        in_specs=(
            P("slab"),
            P("slab", None, "cross"),
            P("slab", "cross", None, None),
            P("slab", "cross"),
            P("slab", "cross", None, None),
            P("slab", "cross"),
        ),
        out_specs=(P("slab", None, "cross"), P("slab", None, "cross")),
        check_vma=False,
    )
```

```python
import functools

import jax
import jax.numpy as jnp
from jax import lax
from jax.experimental import pallas as pl
from jax.experimental.pallas import tpu as pltpu
from jax.sharding import PartitionSpec as P

HB = 4
CHUNKS = 2
ROW_TILE = 16
VMEM = pl.BlockSpec(memory_space=pltpu.VMEM)
SMEM = pl.BlockSpec(memory_space=pltpu.SMEM)
HBM = pl.BlockSpec(memory_space=pltpu.HBM)
ANY = pl.BlockSpec(memory_space=pl.ANY)


def params(mib):
    return pltpu.CompilerParams(vmem_limit_bytes=mib << 20)


def pinned(x, space):
    return pltpu.with_memory_space_constraint(x, space)


def chunk_rows(sources):
    tiles = sources // ROW_TILE
    count = min(CHUNKS, tiles)
    sizes = [(tiles // count + (j < tiles % count)) * ROW_TILE for j in range(count)]
    return [(sum(sizes[:j]), sizes[j]) for j in range(count)]


def is_even():
    return lax.rem(lax.axis_index("cross"), 2) == 0


def in_low_half():
    return lax.axis_index("slab") < lax.axis_size("slab") // 2


def edge_places(halo):
    even = is_even()
    left = pl.multiple_of(jnp.where(even, 0, halo), halo)
    right = pl.multiple_of(jnp.where(even, halo, 0), halo)
    return left, right


def source_kernel(row0, thick_ref, layers_ref, total_ref, edge_ref, *rest):
    *mid, buf, sems = rest
    depth, rows, width = buf.shape
    halo = edge_ref.shape[1] // 2
    thick = thick_ref[0]

    def copy(k):
        return pltpu.make_async_copy(
            layers_ref.at[k, pl.ds(row0, rows), :], buf.at[k], sems.at[k]
        )

    for k in range(depth):
        pl.when(k < thick)(copy(k).start)
    for k in range(depth):
        pl.when(k < thick)(copy(k).wait)
    value = jnp.zeros((rows, width), jnp.float32)
    for k in range(depth):
        value = value + jnp.where(k < thick, buf[k], jnp.bfloat16(0)).astype(jnp.float32)
    total_ref[...] = value
    value = value.astype(jnp.bfloat16)
    left, right = edge_places(halo)
    edge_ref[:, pl.ds(left, halo)] = value[:, :halo]
    edge_ref[:, pl.ds(right, halo)] = value[:, width - halo :]
    if mid:
        mid[0][...] = value[:, halo : width - halo]


def fetch_kernel(low, down_ref, up_ref, after_ref, out_ref, sem):
    del after_ref

    @pl.when(in_low_half() == low)
    def _():
        copy = pltpu.make_async_copy(down_ref.at[0], out_ref, sem)
        copy.start()
        copy.wait()

    @pl.when(in_low_half() != low)
    def _():
        copy = pltpu.make_async_copy(up_ref.at[0], out_ref, sem)
        copy.start()
        copy.wait()


def product_kernel(hop, parts, cols_ref, far_ref, near_ref, *rest):
    ins, (green_ref, total_ref), outs, ext = (
        rest[:parts],
        rest[parts : parts + 2],
        rest[parts + 2 : -1],
        rest[-1],
    )
    width = total_ref.shape[1]
    halo = far_ref.shape[1]
    bsize = green_ref.shape[-1]
    per_dev = width // bsize
    kcount = green_ref.shape[0] // per_dev
    slab = lax.axis_index("slab")
    active = jnp.logical_or(slab == hop, slab == lax.axis_size("slab") - 1 - hop)

    @pl.when(active)
    def _():
        left, right = edge_places(halo)
        ext[:, pl.ds(halo, halo)] = ins[0][:, pl.ds(left, halo)]
        ext[:, pl.ds(width, halo)] = ins[0][:, pl.ds(right, halo)]
        if parts == 2:
            ext[:, 2 * halo : width] = ins[1][...]

        @pl.when(is_even())
        def _():
            ext[:, :halo] = far_ref[...]
            ext[:, halo + width :] = near_ref[...]

        @pl.when(jnp.logical_not(is_even()))
        def _():
            ext[:, :halo] = near_ref[...]
            ext[:, halo + width :] = far_ref[...]

        for i in range(per_dev):
            picked, blocks = [], []
            for k in range(kcount):
                at = pl.multiple_of(cols_ref[0, i * kcount + k] * bsize, bsize)
                picked.append(ext[:, pl.ds(at, bsize)])
                blocks.append(green_ref[i * kcount + k])
            value = lax.dot_general(
                jnp.concatenate(picked, 1),
                jnp.concatenate(blocks, 1),
                (((1,), (1,)), ((), ())),
                preferred_element_type=jnp.float32,
            )
            value = (value + total_ref[:, i * bsize : (i + 1) * bsize]).astype(jnp.bfloat16)
            at = i * bsize
            if at < halo:
                outs[0][:, pl.ds(pl.multiple_of(left + at, bsize), bsize)] = value
            elif at >= width - halo:
                at = at - (width - halo)
                outs[0][:, pl.ds(pl.multiple_of(right + at, bsize), bsize)] = value
            else:
                outs[1][:, at - halo : at - halo + bsize] = value


def store_kernel(hops, pieces, parts, *rest):
    count = len(hops) * len(pieces) * parts
    ins, (down_ref, up_ref, sems) = rest[:count], rest[-3:]
    width = down_ref.shape[2]
    halo = ins[0].shape[1] // 2
    slab = lax.axis_index("slab")
    last = lax.axis_size("slab") - 1

    def copies(h, out_ref, which):
        left, right = edge_places(halo)
        made = []
        for j, (row0, rows) in enumerate(pieces):
            at = (hops.index(h) * len(pieces) + j) * parts
            span = pl.ds(row0, rows)
            moves = [
                (ins[at].at[:, pl.ds(left, halo)], 0, halo),
                (ins[at].at[:, pl.ds(right, halo)], width - halo, halo),
            ]
            if parts == 2:
                moves.append((ins[at + 1], halo, width - 2 * halo))
            for src, col, size in moves:
                dst = out_ref.at[0, span, pl.ds(col, size)]
                made.append(pltpu.make_async_copy(src, dst, sems.at[which, len(made)]))
        return made

    plan = []
    for h in hops:
        plan.append((h, down_ref, 0, slab == h))
        plan.append((h, up_ref, 1, slab == last - h))
    for h, ref, which, chosen in plan:

        @pl.when(chosen)
        def _():
            for copy in copies(h, ref, which):
                copy.start()

    for h, ref, which, chosen in plan:

        @pl.when(chosen)
        def _():
            for copy in copies(h, ref, which):
                copy.wait()


def shards(thickness, layer_sources, green_down, column_down, green_up, column_up):
    slabs = lax.axis_size("slab")
    cross = lax.axis_size("cross")
    lateral = lax.axis_index("cross")
    depth, sources, width = layer_sources.shape
    bsize = green_down.shape[-1]
    per_dev = width // bsize
    total_blocks = per_dev * cross
    nblocks = green_down.shape[1]
    halo = HB * bsize
    chunks = chunk_rows(sources)
    parts = 2 if per_dev > 2 * HB else 1
    layers = pinned(layer_sources, pltpu.HBM)
    greens = (pinned(green_down, pltpu.HBM), pinned(green_up, pltpu.HBM))

    def trace(rows):
        widths = [2 * halo, width - 2 * halo][:parts]
        return [pltpu.VMEM((rows, w), jnp.bfloat16) for w in widths]

    def local(low):
        cols = jnp.where(in_low_half() == low, column_down, column_up)
        return (cols - lateral * per_dev + HB) % total_blocks

    def fetch(low, after):
        return pl.pallas_call(
            functools.partial(fetch_kernel, low),
            out_shape=pltpu.VMEM(green_down.shape[1:], jnp.bfloat16),
            in_specs=[HBM, HBM, ANY],
            out_specs=VMEM,
            scratch_shapes=[pltpu.SemaphoreType.DMA],
            compiler_params=params(8),
            name="fetch",
        )(*greens, after)

    def source(row0, rows):
        return pl.pallas_call(
            functools.partial(source_kernel, row0),
            out_shape=[pltpu.VMEM((rows, width), jnp.float32), *trace(rows)],
            in_specs=[SMEM, HBM],
            out_specs=[VMEM] * (1 + parts),
            scratch_shapes=[
                pltpu.VMEM((depth, rows, width), jnp.bfloat16),
                pltpu.SemaphoreType.DMA((depth,)),
            ],
            compiler_params=params(8),
            name="source",
        )(thickness, layers)

    def product(h, cols, far, near, got, green, total):
        rows = total.shape[0]
        ins = [pinned(x, pltpu.VMEM) for x in (far, near, *got, green, total)]
        return pl.pallas_call(
            functools.partial(product_kernel, h, parts),
            out_shape=trace(rows),
            in_specs=[SMEM] + [VMEM] * len(ins),
            out_specs=[VMEM] * parts,
            scratch_shapes=[pltpu.VMEM((rows, width + 2 * halo), jnp.bfloat16)],
            compiler_params=params(8),
            cost_estimate=pl.CostEstimate(
                flops=2 * rows * nblocks * bsize * bsize,
                bytes_accessed=nblocks * bsize * bsize * 2,
                transcendentals=0,
            ),
            name="product",
        )(cols, *ins)

    def store(hops, pieces, arrays, into=None):
        ins = [pinned(x, pltpu.VMEM) for x in arrays]
        given = [] if into is None else [pinned(x, pltpu.HBM) for x in into]
        return pl.pallas_call(
            functools.partial(store_kernel, hops, pieces, parts),
            out_shape=[pltpu.HBM((1, sources, width), jnp.bfloat16)] * 2,
            in_specs=[VMEM] * len(ins) + [HBM] * len(given),
            out_specs=[HBM, HBM],
            scratch_shapes=[pltpu.SemaphoreType.DMA((2, len(pieces) * (1 + parts)))],
            input_output_aliases={len(ins) + i: i for i in range(len(given))},
            compiler_params=params(4),
            name="store",
        )(*ins, *given)

    def mate(c):
        return c ^ 1

    def next_chip(c):
        return (c + 1) % cross if c % 2 else (c - 1) % cross

    def hop(x, h):
        there = {s: s for s in range(slabs)}
        for a, b in ((h - 1, h), (slabs - h, slabs - 1 - h)):
            there[a], there[b] = b, a
        route = []
        for s in range(slabs):
            for c in range(cross):
                to = c if there[s] != s else mate(c)
                route.append((s * cross + c, there[s] * cross + to))
        return lax.ppermute(x, ("slab", "cross"), route)

    def to_mate(x):
        return lax.ppermute(x, "cross", [(c, mate(c)) for c in range(cross)])

    def to_next_chip(x, h):
        route = []
        for s in range(slabs):
            for c in range(cross):
                to = next_chip(c) if s in (h, slabs - 1 - h) else mate(c)
                route.append((s * cross + c, s * cross + to))
        return lax.ppermute(x, ("slab", "cross"), route)

    totals, made = [], {}
    for j, (row0, rows) in enumerate(chunks):
        total, *out = source(row0, rows)
        totals.append(total)
        made[0, j] = out
    cols = {low: local(low) for low in (True, False)}
    green = {}
    order = sorted(
        ((h, j) for h in range(1, slabs) for j in range(len(chunks))),
        key=lambda hj: (hj[0] + hj[1], hj[0]),
    )
    for h, j in order:
        got = [hop(x, h) for x in made[h - 1, j]]
        far = to_next_chip(got[0][:, :halo], h)
        near = to_mate(got[0][:, halo:])
        low = h < slabs // 2
        which = (low, h == slabs - 1)
        if which not in green:
            green[which] = fetch(low, got[0])
        made[h, j] = product(h, cols[low], far, near, got, green[which], totals[j])

    early = list(range(slabs - 1))
    outs = store(early, chunks, [x for h in early for j in range(len(chunks)) for x in made[h, j]])
    for j, piece in enumerate(chunks):
        outs = store([slabs - 1], [piece], made[slabs - 1, j], outs)
    return tuple(outs)


def solution(mesh):
    return jax.shard_map(
        shards,
        mesh=mesh,
        in_specs=(
            P("slab"),
            P("slab", None, "cross"),
            P("slab", "cross", None, None),
            P("slab", "cross"),
            P("slab", "cross", None, None),
            P("slab", "cross"),
        ),
        out_specs=(P("slab", None, "cross"), P("slab", None, "cross")),
        check_vma=False,
    )
```

```python
import functools

import jax
import jax.numpy as jnp
from jax import lax
from jax.experimental import pallas as pl
from jax.experimental.pallas import tpu as pltpu
from jax.sharding import PartitionSpec as P

HB = 4
CHUNKS = 2
CP = 1000
SPLIT = ((1, 1), (1, 1), (0, 1))
ROW_TILE = 16
VMEM = pl.BlockSpec(memory_space=pltpu.VMEM)
SMEM = pl.BlockSpec(memory_space=pltpu.SMEM)
HBM = pl.BlockSpec(memory_space=pltpu.HBM)
ANY = pl.BlockSpec(memory_space=pl.ANY)


def params(mib):
    return pltpu.CompilerParams(vmem_limit_bytes=mib << 20)


def pinned(x, space):
    return pltpu.with_memory_space_constraint(x, space)


def chunk_rows(sources):
    tiles = sources // ROW_TILE
    count = min(CHUNKS, tiles)
    sizes = [(tiles // count + (j < tiles % count)) * ROW_TILE for j in range(count)]
    return [(sum(sizes[:j]), sizes[j]) for j in range(count)]


def is_even():
    return lax.rem(lax.axis_index("cross"), 2) == 0


def in_low_half():
    return lax.axis_index("slab") < lax.axis_size("slab") // 2


def edge_places(halo):
    even = is_even()
    left = pl.multiple_of(jnp.where(even, 0, halo), halo)
    right = pl.multiple_of(jnp.where(even, halo, 0), halo)
    return left, right


def source_kernel(row0, halo, thick_ref, layers_ref, total_ref, edge_ref, *rest):
    *mid, buf, sems = rest
    depth, rows, width = buf.shape
    thick = thick_ref[0]

    def copy(k):
        return pltpu.make_async_copy(
            layers_ref.at[k, pl.ds(row0, rows), :], buf.at[k], sems.at[k]
        )

    for k in range(depth):
        pl.when(k < thick)(copy(k).start)
    for k in range(depth):
        pl.when(k < thick)(copy(k).wait)
    value = jnp.zeros((rows, width), jnp.float32)
    for k in range(depth):
        value = value + jnp.where(k < thick, buf[k], jnp.bfloat16(0)).astype(jnp.float32)
    total_ref[...] = value
    value = value.astype(jnp.bfloat16)
    left, right = edge_places(halo)
    edge_ref[:, pl.ds(left, halo)] = value[:, :halo]
    edge_ref[:, pl.ds(right, halo)] = value[:, width - halo :]
    if mid:
        mid[0][...] = value[:, halo : width - halo]
    elif width > 2 * halo:
        edge_ref[:, 2 * halo :] = value[:, halo : width - halo]


def fetch_kernel(hops, low, down_ref, up_ref, out_ref, sem):
    slab, last = lax.axis_index("slab"), lax.axis_size("slab") - 1
    used = functools.reduce(jnp.logical_or, [(slab == h) | (slab == last - h) for h in hops])

    @pl.when(used & (in_low_half() == low))
    def _():
        copy = pltpu.make_async_copy(down_ref.at[0], out_ref, sem)
        copy.start()
        copy.wait()

    @pl.when(used & (in_low_half() != low))
    def _():
        copy = pltpu.make_async_copy(up_ref.at[0], out_ref, sem)
        copy.start()
        copy.wait()


def product_kernel(hop, parts, split, cols_ref, far_ref, near_ref, *rest):
    ins, (green_ref, total_ref), outs, ext = (
        rest[:parts],
        rest[parts : parts + 2],
        rest[parts + 2 : -1],
        rest[-1],
    )
    width = total_ref.shape[1]
    halo = far_ref.shape[1]
    bsize = green_ref.shape[-1]
    per_dev = width // bsize
    kcount = green_ref.shape[0] // per_dev
    slab = lax.axis_index("slab")
    active = jnp.logical_or(slab == hop, slab == lax.axis_size("slab") - 1 - hop)

    @pl.when(active)
    def _():
        left, right = edge_places(halo)
        ext[:, pl.ds(halo, halo)] = ins[0][:, pl.ds(left, halo)]
        ext[:, pl.ds(width, halo)] = ins[0][:, pl.ds(right, halo)]
        if parts == 2:
            ext[:, 2 * halo : width] = ins[1][...]
        elif width > 2 * halo:
            ext[:, 2 * halo : width] = ins[0][:, 2 * halo :]

        @pl.when(is_even())
        def _():
            ext[:, :halo] = far_ref[...]
            ext[:, halo + width :] = near_ref[...]

        @pl.when(jnp.logical_not(is_even()))
        def _():
            ext[:, :halo] = near_ref[...]
            ext[:, halo + width :] = far_ref[...]

        for i in range(per_dev):
            picked, blocks = [], []
            for k in range(kcount):
                at = pl.multiple_of(cols_ref[0, i * kcount + k] * bsize, bsize)
                picked.append(ext[:, pl.ds(at, bsize)])
                blocks.append(green_ref[i * kcount + k])
            value = lax.dot_general(
                jnp.concatenate(picked, 1),
                jnp.concatenate(blocks, 1),
                (((1,), (1,)), ((), ())),
                preferred_element_type=jnp.float32,
            )
            value = (value + total_ref[:, i * bsize : (i + 1) * bsize]).astype(jnp.bfloat16)
            at = i * bsize
            if at < halo:
                outs[0][:, pl.ds(pl.multiple_of(left + at, bsize), bsize)] = value
            elif at >= width - halo:
                at = at - (width - halo)
                outs[0][:, pl.ds(pl.multiple_of(right + at, bsize), bsize)] = value
            elif split:
                outs[1][:, at - halo : at - halo + bsize] = value
            else:
                outs[0][:, at + halo : at + halo + bsize] = value


def store_kernel(halo, hops, pieces, splits, given, *rest):
    ins, (down_ref, up_ref, done_ref, sems) = list(rest[: -4 - given]), rest[-4:]
    done_ref[...] = jnp.zeros_like(done_ref)
    width = down_ref.shape[2]
    slab = lax.axis_index("slab")
    last = lax.axis_size("slab") - 1
    traces = {}
    splits = list(splits)
    for h in hops:
        for j in range(len(pieces)):
            traces[h, j] = [ins.pop(0) for _ in range(1 + splits.pop(0))]

    def copies(h, out_ref, which):
        left, right = edge_places(halo)
        made = []
        for j, (row0, rows) in enumerate(pieces):
            edge, *mid = traces[h, j]
            moves = [
                (edge.at[:, pl.ds(left, halo)], 0, halo),
                (edge.at[:, pl.ds(right, halo)], width - halo, halo),
            ]
            size = width - 2 * halo
            if mid:
                moves.append((mid[0], halo, size))
            elif size:
                moves.append((edge.at[:, pl.ds(2 * halo, size)], halo, size))
            for src, col, size in moves:
                dst = out_ref.at[0, pl.ds(row0, rows), pl.ds(col, size)]
                made.append(pltpu.make_async_copy(src, dst, sems.at[which, len(made)]))
        return made

    plan = []
    for h in hops:
        plan.append((h, down_ref, 0, slab == h))
        plan.append((h, up_ref, 1, slab == last - h))
    for h, ref, which, chosen in plan:

        @pl.when(chosen)
        def _():
            for copy in copies(h, ref, which):
                copy.start()

    for h, ref, which, chosen in plan:

        @pl.when(chosen)
        def _():
            for copy in copies(h, ref, which):
                copy.wait()


def shards(thickness, layer_sources, green_down, column_down, green_up, column_up):
    slabs = lax.axis_size("slab")
    cross = lax.axis_size("cross")
    lateral = lax.axis_index("cross")
    depth, sources, width = layer_sources.shape
    bsize = green_down.shape[-1]
    per_dev = width // bsize
    total_blocks = per_dev * cross
    nblocks = green_down.shape[1]
    halo = HB * bsize
    chunks = chunk_rows(sources)

    layers = pinned(layer_sources, pltpu.HBM)
    greens = (pinned(green_down, pltpu.HBM), pinned(green_up, pltpu.HBM))

    def splits(h, j):
        return int(per_dev > 2 * HB and SPLIT[min(h * 3 // (slabs - 1), 2)][min(j, 1)])

    token = []

    def launch(kernel, ins, in_specs, out_shape, out_specs, scratch, mib, name, aliases=None):
        count = len(ins)
        ins, in_specs = [*ins, *token], [*in_specs, *[ANY] * len(token)]
        given = len(ins)

        def body(*refs):
            kernel(*refs[:count], *refs[given:])

        out = pl.pallas_call(
            body,
            out_shape=out_shape,
            in_specs=in_specs,
            out_specs=out_specs,
            scratch_shapes=scratch,
            input_output_aliases=aliases or {},
            compiler_params=params(mib),
            name=name,
        )(*ins)
        token[:] = [out[-1]]
        return out

    def trace(rows, split):
        widths = [2 * halo, width - 2 * halo] if split else [width]
        return [pltpu.VMEM((rows, w), jnp.bfloat16) for w in widths]

    def local(low):
        cols = jnp.where(in_low_half() == low, column_down, column_up)
        return (cols - lateral * per_dev + HB) % total_blocks

    def fetch(hops):
        (block,) = launch(
            functools.partial(fetch_kernel, hops, hops[0] < slabs // 2),
            greens,
            [HBM, HBM],
            [pltpu.VMEM(green_down.shape[1:], jnp.bfloat16)],
            [VMEM],
            [pltpu.SemaphoreType.DMA],
            8,
            "fetch",
        )
        return block

    def source(j, row0, rows):
        out_shape = [pltpu.VMEM((rows, width), jnp.float32), *trace(rows, splits(0, j))]
        total, *out = launch(
            functools.partial(source_kernel, row0, halo),
            [thickness, layers],
            [SMEM, HBM],
            out_shape,
            [VMEM] * len(out_shape),
            [pltpu.VMEM((depth, rows, width), jnp.bfloat16), pltpu.SemaphoreType.DMA((depth,))],
            8,
            "source",
        )
        return total, *out

    def product(h, j, cols, far, near, got, green, total):
        rows = total.shape[0]
        ins = [pinned(x, pltpu.VMEM) for x in (far, near, *got, green, total)]
        out_shape = trace(rows, splits(h, j))
        return launch(
            functools.partial(product_kernel, h, len(got), len(out_shape) == 2),
            [cols, *ins],
            [SMEM] + [VMEM] * len(ins),
            out_shape,
            [VMEM] * len(out_shape),
            [pltpu.VMEM((rows, width + 2 * halo), jnp.bfloat16)],
            8,
            "product",
        )

    def store(hops, j0, pieces, arrays, into=()):
        ins = [pinned(x, pltpu.VMEM) for x in arrays]
        given = [pinned(x, pltpu.HBM) for x in into]
        *outs, _ = launch(
            functools.partial(
                store_kernel,
                halo,
                hops,
                pieces,
                [splits(h, j0 + j) for h in hops for j in range(len(pieces))],
                len(given),
            ),
            [*ins, *given],
            [VMEM] * len(ins) + [HBM] * len(given),
            [pltpu.HBM((1, sources, width), jnp.bfloat16)] * 2
            + [pltpu.VMEM((8, 128), jnp.float32)],
            [HBM, HBM, VMEM],
            [pltpu.SemaphoreType.DMA((2, len(pieces) * 3))],
            4,
            "store",
            {len(ins) + i: i for i in range(len(given))},
        )
        return outs

    def mate(c):
        return c ^ 1

    def next_chip(c):
        return (c + 1) % cross if c % 2 else (c - 1) % cross

    def hop(x, h):
        there = {s: s for s in range(slabs)}
        for a, b in ((h - 1, h), (slabs - h, slabs - 1 - h)):
            there[a], there[b] = b, a
        route = []
        for s in range(slabs):
            for c in range(cross):
                to = c if there[s] != s else mate(c)
                route.append((s * cross + c, there[s] * cross + to))
        return lax.ppermute(x, ("slab", "cross"), route)

    def to_mate(x):
        return lax.ppermute(x, "cross", [(c, mate(c)) for c in range(cross)])

    def to_next_chip(x, h):
        route = []
        for s in range(slabs):
            for c in range(cross):
                to = next_chip(c) if s in (h, slabs - 1 - h) else mate(c)
                route.append((s * cross + c, s * cross + to))
        return lax.ppermute(x, ("slab", "cross"), route)

    totals, made, moved = [], {}, {}
    for j, (row0, rows) in enumerate(chunks):
        total, *out = source(j, row0, rows)
        totals.append(total)
        made[0, j] = out
    cols = {low: local(low) for low in (True, False)}
    green = {}
    order = sorted(
        ((h, j) for h in range(1, slabs) for j in range(len(chunks))),
        key=lambda hj: (hj[0] + hj[1], hj[0]),
    )
    early = list(range(slabs - 1))
    groups = [list(range(1, slabs // 2)), list(range(slabs // 2, slabs - 1)), [slabs - 1]]
    groups = [g for g in groups if g]
    group_of = {h: g for g in range(len(groups)) for h in groups[g]}
    early = list(range(slabs - 1))
    outs, sides = [], {}

    def lateral(h, j):
        if (h, j) not in sides:
            edges = moved[h, j][0][:, : 2 * halo]
            if h == slabs - 1 and j:
                edges, _ = lax.optimization_barrier((edges, made[h, j - 1][0]))
            sides[h, j] = (to_next_chip(edges[:, :halo], h), to_mate(edges[:, halo:]))
        return sides[h, j]

    def send(h, j):
        moved[h, j] = [hop(x, h) for x in made[h - 1, j]]

    for j in range(len(chunks)):
        send(1, j)
    for h, j in order:
        far, near = lateral(h, j)
        g = group_of[h]
        for ahead in range(g + 1 + (g + 1 < min(2, len(groups)))):
            if ahead not in green:
                green[ahead] = fetch(groups[ahead])
        if h == slabs - 1 and j == 0:
            arrays = [x for a in early for b in range(len(chunks)) for x in made[a, b]]
            outs = store(early, 0, chunks, arrays)
        made[h, j] = product(
            h, j, cols[h < slabs // 2], far, near, moved[h, j], green[g], totals[j]
        )
        if h < slabs - 1:
            send(h + 1, j)
        else:
            outs = store([h], j, [chunks[j]], made[h, j], outs)
        if (h, j) == (slabs - 2, 0) and len(groups) - 1 not in green:
            green[len(groups) - 1] = fetch(groups[-1])
    return tuple(outs)


def solution(mesh):
    return jax.shard_map(
        shards,
        mesh=mesh,
        in_specs=(
            P("slab"),
            P("slab", None, "cross"),
            P("slab", "cross", None, None),
            P("slab", "cross"),
            P("slab", "cross", None, None),
            P("slab", "cross"),
        ),
        out_specs=(P("slab", None, "cross"), P("slab", None, "cross")),
        check_vma=False,
    )
```

```python
import functools

import jax
import jax.numpy as jnp
from jax import lax
from jax.experimental import pallas as pl
from jax.experimental.pallas import tpu as pltpu
from jax.sharding import PartitionSpec as P

HB = 4
CHUNKS = 2
CP = 1000
SPLIT = ((1, 1), (1, 1), (0, 1))
ROW_TILE = 16
VMEM = pl.BlockSpec(memory_space=pltpu.VMEM)
SMEM = pl.BlockSpec(memory_space=pltpu.SMEM)
HBM = pl.BlockSpec(memory_space=pltpu.HBM)
ANY = pl.BlockSpec(memory_space=pl.ANY)


def params(mib):
    return pltpu.CompilerParams(vmem_limit_bytes=mib << 20)


def pinned(x, space):
    return pltpu.with_memory_space_constraint(x, space)


def chunk_rows(sources):
    tiles = sources // ROW_TILE
    count = min(CHUNKS, tiles)
    sizes = [(tiles // count + (j < tiles % count)) * ROW_TILE for j in range(count)]
    return [(sum(sizes[:j]), sizes[j]) for j in range(count)]


def is_even():
    return lax.rem(lax.axis_index("cross"), 2) == 0


def in_low_half():
    return lax.axis_index("slab") < lax.axis_size("slab") // 2


def edge_places(halo):
    even = is_even()
    left = pl.multiple_of(jnp.where(even, 0, halo), halo)
    right = pl.multiple_of(jnp.where(even, halo, 0), halo)
    return left, right


def source_kernel(row0, halo, thick_ref, layers_ref, total_ref, edge_ref, *rest):
    *mid, buf, sems = rest
    depth, rows, width = buf.shape
    thick = thick_ref[0]

    def copy(k):
        return pltpu.make_async_copy(
            layers_ref.at[k, pl.ds(row0, rows), :], buf.at[k], sems.at[k]
        )

    for k in range(depth):
        pl.when(k < thick)(copy(k).start)
    for k in range(depth):
        pl.when(k < thick)(copy(k).wait)
    value = jnp.zeros((rows, width), jnp.float32)
    for k in range(depth):
        value = value + jnp.where(k < thick, buf[k], jnp.bfloat16(0)).astype(jnp.float32)
    total_ref[...] = value
    value = value.astype(jnp.bfloat16)
    left, right = edge_places(halo)
    edge_ref[:, pl.ds(left, halo)] = value[:, :halo]
    edge_ref[:, pl.ds(right, halo)] = value[:, width - halo :]
    if mid:
        mid[0][...] = value[:, halo : width - halo]
    elif width > 2 * halo:
        edge_ref[:, 2 * halo :] = value[:, halo : width - halo]


def fetch_kernel(hops, low, down_ref, up_ref, out_ref, sem):
    slab, last = lax.axis_index("slab"), lax.axis_size("slab") - 1
    used = functools.reduce(jnp.logical_or, [(slab == h) | (slab == last - h) for h in hops])

    @pl.when(used & (in_low_half() == low))
    def _():
        copy = pltpu.make_async_copy(down_ref.at[0], out_ref, sem)
        copy.start()
        copy.wait()

    @pl.when(used & (in_low_half() != low))
    def _():
        copy = pltpu.make_async_copy(up_ref.at[0], out_ref, sem)
        copy.start()
        copy.wait()


def last_product_kernel(hop, parts, row0, cols_ref, far_ref, near_ref, *rest):
    ins = rest[: parts + 2]
    down_ref, up_ref, done_ref, ext, held, sems = rest[parts + 4 :]
    rows, width = held.shape
    count = sems.shape[1]
    size = width // count
    goes_down = lax.axis_index("slab") == hop
    goes_up = lax.axis_index("slab") == lax.axis_size("slab") - 1 - hop
    done_ref[...] = jnp.zeros_like(done_ref)

    def copy(ref, which, n):
        span = pl.ds(n * size, size)
        return pltpu.make_async_copy(
            held.at[:, span], ref.at[0, pl.ds(row0, rows), span], sems.at[which, n]
        )

    def emit(at, value):
        held[:, at : at + value.shape[1]] = value
        n, part = divmod(at + value.shape[1], size)
        if part == 0:
            pl.when(goes_down)(copy(down_ref, 0, n - 1).start)
            pl.when(goes_up)(copy(up_ref, 1, n - 1).start)

    product_kernel(hop, parts, False, cols_ref, far_ref, near_ref, *ins, ext, emit=emit)
    for n in range(count):
        pl.when(goes_down)(copy(down_ref, 0, n).wait)
        pl.when(goes_up)(copy(up_ref, 1, n).wait)


def product_kernel(hop, parts, split, cols_ref, far_ref, near_ref, *rest, emit=None):
    ins, (green_ref, total_ref), outs, ext = (
        rest[:parts],
        rest[parts : parts + 2],
        rest[parts + 2 : -1],
        rest[-1],
    )
    width = total_ref.shape[1]
    halo = far_ref.shape[1]
    bsize = green_ref.shape[-1]
    per_dev = width // bsize
    kcount = green_ref.shape[0] // per_dev
    slab = lax.axis_index("slab")
    active = jnp.logical_or(slab == hop, slab == lax.axis_size("slab") - 1 - hop)

    @pl.when(active)
    def _():
        left, right = edge_places(halo)
        ext[:, pl.ds(halo, halo)] = ins[0][:, pl.ds(left, halo)]
        ext[:, pl.ds(width, halo)] = ins[0][:, pl.ds(right, halo)]
        if parts == 2:
            ext[:, 2 * halo : width] = ins[1][...]
        elif width > 2 * halo:
            ext[:, 2 * halo : width] = ins[0][:, 2 * halo :]

        @pl.when(is_even())
        def _():
            ext[:, :halo] = far_ref[...]
            ext[:, halo + width :] = near_ref[...]

        @pl.when(jnp.logical_not(is_even()))
        def _():
            ext[:, :halo] = near_ref[...]
            ext[:, halo + width :] = far_ref[...]

        for i in range(per_dev):
            picked, blocks = [], []
            for k in range(kcount):
                at = pl.multiple_of(cols_ref[0, i * kcount + k] * bsize, bsize)
                picked.append(ext[:, pl.ds(at, bsize)])
                blocks.append(green_ref[i * kcount + k])
            value = lax.dot_general(
                jnp.concatenate(picked, 1),
                jnp.concatenate(blocks, 1),
                (((1,), (1,)), ((), ())),
                preferred_element_type=jnp.float32,
            )
            value = (value + total_ref[:, i * bsize : (i + 1) * bsize]).astype(jnp.bfloat16)
            at = i * bsize
            if emit:
                emit(at, value)
            elif at < halo:
                outs[0][:, pl.ds(pl.multiple_of(left + at, bsize), bsize)] = value
            elif at >= width - halo:
                at = at - (width - halo)
                outs[0][:, pl.ds(pl.multiple_of(right + at, bsize), bsize)] = value
            elif split:
                outs[1][:, at - halo : at - halo + bsize] = value
            else:
                outs[0][:, at + halo : at + halo + bsize] = value


def store_kernel(halo, hops, pieces, splits, given, *rest):
    ins, (down_ref, up_ref, done_ref, sems) = list(rest[: -4 - given]), rest[-4:]
    done_ref[...] = jnp.zeros_like(done_ref)
    width = down_ref.shape[2]
    slab = lax.axis_index("slab")
    last = lax.axis_size("slab") - 1
    traces = {}
    splits = list(splits)
    for h in hops:
        for j in range(len(pieces)):
            traces[h, j] = [ins.pop(0) for _ in range(1 + splits.pop(0))]

    def copies(h, out_ref, which):
        left, right = edge_places(halo)
        made = []
        for j, (row0, rows) in enumerate(pieces):
            edge, *mid = traces[h, j]
            moves = [
                (edge.at[:, pl.ds(left, halo)], 0, halo),
                (edge.at[:, pl.ds(right, halo)], width - halo, halo),
            ]
            size = width - 2 * halo
            if mid:
                moves.append((mid[0], halo, size))
            elif size:
                moves.append((edge.at[:, pl.ds(2 * halo, size)], halo, size))
            for src, col, size in moves:
                dst = out_ref.at[0, pl.ds(row0, rows), pl.ds(col, size)]
                made.append(pltpu.make_async_copy(src, dst, sems.at[which, len(made)]))
        return made

    plan = []
    for h in hops:
        plan.append((h, down_ref, 0, slab == h))
        plan.append((h, up_ref, 1, slab == last - h))
    for h, ref, which, chosen in plan:

        @pl.when(chosen)
        def _():
            for copy in copies(h, ref, which):
                copy.start()

    for h, ref, which, chosen in plan:

        @pl.when(chosen)
        def _():
            for copy in copies(h, ref, which):
                copy.wait()


def shards(thickness, layer_sources, green_down, column_down, green_up, column_up):
    slabs = lax.axis_size("slab")
    cross = lax.axis_size("cross")
    lateral = lax.axis_index("cross")
    depth, sources, width = layer_sources.shape
    bsize = green_down.shape[-1]
    per_dev = width // bsize
    total_blocks = per_dev * cross
    nblocks = green_down.shape[1]
    halo = HB * bsize
    chunks = chunk_rows(sources)

    layers = pinned(layer_sources, pltpu.HBM)
    greens = (pinned(green_down, pltpu.HBM), pinned(green_up, pltpu.HBM))

    def splits(h, j):
        return int(per_dev > 2 * HB and SPLIT[min(h * 3 // (slabs - 1), 2)][min(j, 1)])

    token = []

    def launch(kernel, ins, in_specs, out_shape, out_specs, scratch, mib, name, aliases=None):
        count = len(ins)
        ins, in_specs = [*ins, *token], [*in_specs, *[ANY] * len(token)]
        given = len(ins)

        def body(*refs):
            kernel(*refs[:count], *refs[given:])

        out = pl.pallas_call(
            body,
            out_shape=out_shape,
            in_specs=in_specs,
            out_specs=out_specs,
            scratch_shapes=scratch,
            input_output_aliases=aliases or {},
            compiler_params=params(mib),
            name=name,
        )(*ins)
        token[:] = [out[-1]]
        return out

    def trace(rows, split):
        widths = [2 * halo, width - 2 * halo] if split else [width]
        return [pltpu.VMEM((rows, w), jnp.bfloat16) for w in widths]

    def local(low):
        cols = jnp.where(in_low_half() == low, column_down, column_up)
        return (cols - lateral * per_dev + HB) % total_blocks

    def fetch(hops):
        (block,) = launch(
            functools.partial(fetch_kernel, hops, hops[0] < slabs // 2),
            greens,
            [HBM, HBM],
            [pltpu.VMEM(green_down.shape[1:], jnp.bfloat16)],
            [VMEM],
            [pltpu.SemaphoreType.DMA],
            8,
            "fetch",
        )
        return block

    def source(j, row0, rows):
        out_shape = [pltpu.VMEM((rows, width), jnp.float32), *trace(rows, splits(0, j))]
        total, *out = launch(
            functools.partial(source_kernel, row0, halo),
            [thickness, layers],
            [SMEM, HBM],
            out_shape,
            [VMEM] * len(out_shape),
            [pltpu.VMEM((depth, rows, width), jnp.bfloat16), pltpu.SemaphoreType.DMA((depth,))],
            8,
            "source",
        )
        return total, *out

    def product(h, j, cols, far, near, got, green, total):
        rows = total.shape[0]
        ins = [pinned(x, pltpu.VMEM) for x in (far, near, *got, green, total)]
        out_shape = trace(rows, splits(h, j))
        return launch(
            functools.partial(product_kernel, h, len(got), len(out_shape) == 2),
            [cols, *ins],
            [SMEM] + [VMEM] * len(ins),
            out_shape,
            [VMEM] * len(out_shape),
            [pltpu.VMEM((rows, width + 2 * halo), jnp.bfloat16)],
            8,
            "product",
        )

    def last_product(j, cols, far, near, got, green, total, into):
        rows = total.shape[0]
        ins = [pinned(x, pltpu.VMEM) for x in (far, near, *got, green, total)]
        pieces = 4 if per_dev % 4 == 0 else 1
        return launch(
            functools.partial(last_product_kernel, slabs - 1, len(got), chunks[j][0]),
            [cols, *ins, *[pinned(x, pltpu.HBM) for x in into]],
            [SMEM] + [VMEM] * len(ins) + [HBM] * 2,
            [pltpu.HBM((1, sources, width), jnp.bfloat16)] * 2
            + [pltpu.VMEM((8, 128), jnp.float32)],
            [HBM, HBM, VMEM],
            [
                pltpu.VMEM((rows, width + 2 * halo), jnp.bfloat16),
                pltpu.VMEM((rows, width), jnp.bfloat16),
                pltpu.SemaphoreType.DMA((2, pieces)),
            ],
            8,
            "product",
            {len(ins) + 1: 0, len(ins) + 2: 1},
        )[:2]

    def store(hops, j0, pieces, arrays, into=()):
        ins = [pinned(x, pltpu.VMEM) for x in arrays]
        given = [pinned(x, pltpu.HBM) for x in into]
        *outs, _ = launch(
            functools.partial(
                store_kernel,
                halo,
                hops,
                pieces,
                [splits(h, j0 + j) for h in hops for j in range(len(pieces))],
                len(given),
            ),
            [*ins, *given],
            [VMEM] * len(ins) + [HBM] * len(given),
            [pltpu.HBM((1, sources, width), jnp.bfloat16)] * 2
            + [pltpu.VMEM((8, 128), jnp.float32)],
            [HBM, HBM, VMEM],
            [pltpu.SemaphoreType.DMA((2, len(pieces) * 3))],
            4,
            "store",
            {len(ins) + i: i for i in range(len(given))},
        )
        return outs

    def mate(c):
        return c ^ 1

    def next_chip(c):
        return (c + 1) % cross if c % 2 else (c - 1) % cross

    def hop(x, h):
        there = {s: s for s in range(slabs)}
        for a, b in ((h - 1, h), (slabs - h, slabs - 1 - h)):
            there[a], there[b] = b, a
        route = []
        for s in range(slabs):
            for c in range(cross):
                to = c if there[s] != s else mate(c)
                route.append((s * cross + c, there[s] * cross + to))
        return lax.ppermute(x, ("slab", "cross"), route)

    def to_mate(x):
        return lax.ppermute(x, "cross", [(c, mate(c)) for c in range(cross)])

    def to_next_chip(x, h):
        route = []
        for s in range(slabs):
            for c in range(cross):
                to = next_chip(c) if s in (h, slabs - 1 - h) else mate(c)
                route.append((s * cross + c, s * cross + to))
        return lax.ppermute(x, ("slab", "cross"), route)

    totals, made, moved = [], {}, {}
    for j, (row0, rows) in enumerate(chunks):
        total, *out = source(j, row0, rows)
        totals.append(total)
        made[0, j] = out
    cols = {low: local(low) for low in (True, False)}
    green = {}
    order = sorted(
        ((h, j) for h in range(1, slabs) for j in range(len(chunks))),
        key=lambda hj: (hj[0] + hj[1], hj[0]),
    )
    early = list(range(slabs - 1))
    groups = [list(range(1, slabs // 2)), list(range(slabs // 2, slabs - 1)), [slabs - 1]]
    groups = [g for g in groups if g]
    group_of = {h: g for g in range(len(groups)) for h in groups[g]}
    early = list(range(slabs - 1))
    outs, sides = [], {}

    def lateral(h, j):
        if (h, j) not in sides:
            edges = moved[h, j][0][:, : 2 * halo]
            if h == slabs - 1 and j:
                edges, _ = lax.optimization_barrier((edges, sides[h, j - 1][0]))
            sides[h, j] = (to_next_chip(edges[:, :halo], h), to_mate(edges[:, halo:]))
        return sides[h, j]

    def send(h, j):
        moved[h, j] = [hop(x, h) for x in made[h - 1, j]]

    for j in range(len(chunks)):
        send(1, j)
    for h, j in order:
        far, near = lateral(h, j)
        g = group_of[h]
        for ahead in range(g + 1 + (g + 1 < min(2, len(groups)))):
            if ahead not in green:
                green[ahead] = fetch(groups[ahead])
        if h == slabs - 1 and j == 0:
            arrays = [x for a in early for b in range(len(chunks)) for x in made[a, b]]
            outs = store(early, 0, chunks, arrays)
        given = (cols[h < slabs // 2], far, near, moved[h, j], green[g], totals[j])
        if h == slabs - 1:
            outs = last_product(j, *given, outs)
        else:
            made[h, j] = product(h, j, *given)
            send(h + 1, j)
        if (h, j) == (slabs - 2, 0) and len(groups) - 1 not in green:
            green[len(groups) - 1] = fetch(groups[-1])
    return tuple(outs)


def solution(mesh):
    return jax.shard_map(
        shards,
        mesh=mesh,
        in_specs=(
            P("slab"),
            P("slab", None, "cross"),
            P("slab", "cross", None, None),
            P("slab", "cross"),
            P("slab", "cross", None, None),
            P("slab", "cross"),
        ),
        out_specs=(P("slab", None, "cross"), P("slab", None, "cross")),
        check_vma=False,
    )
```

```python
import functools

import jax
import jax.numpy as jnp
from jax import lax
from jax.experimental import pallas as pl
from jax.experimental.pallas import tpu as pltpu
from jax.sharding import PartitionSpec as P

HB = 4
CHUNKS = 2
CP = 1000
SPLIT = ((1, 1), (1, 1), (0, 1))
ROW_TILE = 16
VMEM = pl.BlockSpec(memory_space=pltpu.VMEM)
SMEM = pl.BlockSpec(memory_space=pltpu.SMEM)
HBM = pl.BlockSpec(memory_space=pltpu.HBM)
ANY = pl.BlockSpec(memory_space=pl.ANY)


def params(mib):
    return pltpu.CompilerParams(vmem_limit_bytes=mib << 20)


def pinned(x, space):
    return pltpu.with_memory_space_constraint(x, space)


def chunk_rows(sources):
    tiles = sources // ROW_TILE
    count = min(CHUNKS, tiles)
    sizes = [(tiles // count + (j < tiles % count)) * ROW_TILE for j in range(count)]
    return [(sum(sizes[:j]), sizes[j]) for j in range(count)]


def is_even():
    return lax.rem(lax.axis_index("cross"), 2) == 0


def in_low_half():
    return lax.axis_index("slab") < lax.axis_size("slab") // 2


def edge_places(halo):
    even = is_even()
    left = pl.multiple_of(jnp.where(even, 0, halo), halo)
    right = pl.multiple_of(jnp.where(even, halo, 0), halo)
    return left, right


def source_kernel(row0, halo, thick_ref, layers_ref, total_ref, edge_ref, *rest):
    *mid, buf, sems = rest
    depth, rows, width = buf.shape
    thick = thick_ref[0]

    def copy(k):
        return pltpu.make_async_copy(
            layers_ref.at[k, pl.ds(row0, rows), :], buf.at[k], sems.at[k]
        )

    for k in range(depth):
        pl.when(k < thick)(copy(k).start)
    for k in range(depth):
        pl.when(k < thick)(copy(k).wait)
    value = jnp.zeros((rows, width), jnp.float32)
    for k in range(depth):
        value = value + jnp.where(k < thick, buf[k], jnp.bfloat16(0)).astype(jnp.float32)
    total_ref[...] = value
    value = value.astype(jnp.bfloat16)
    left, right = edge_places(halo)
    edge_ref[:, pl.ds(left, halo)] = value[:, :halo]
    edge_ref[:, pl.ds(right, halo)] = value[:, width - halo :]
    if mid:
        mid[0][...] = value[:, halo : width - halo]
    elif width > 2 * halo:
        edge_ref[:, 2 * halo :] = value[:, halo : width - halo]


def fetch_kernel(hops, low, down_ref, up_ref, out_ref, sem):
    slab, last = lax.axis_index("slab"), lax.axis_size("slab") - 1
    used = functools.reduce(jnp.logical_or, [(slab == h) | (slab == last - h) for h in hops])

    @pl.when(used & (in_low_half() == low))
    def _():
        copy = pltpu.make_async_copy(down_ref.at[0], out_ref, sem)
        copy.start()
        copy.wait()

    @pl.when(used & (in_low_half() != low))
    def _():
        copy = pltpu.make_async_copy(up_ref.at[0], out_ref, sem)
        copy.start()
        copy.wait()


def last_product_kernel(hop, parts, row0, cols_ref, far_ref, near_ref, *rest):
    ins = rest[: parts + 2]
    down_ref, up_ref, done_ref, ext, held, sems = rest[parts + 4 :]
    rows, width = held.shape
    count = sems.shape[1]
    size = width // count
    goes_down = lax.axis_index("slab") == hop
    goes_up = lax.axis_index("slab") == lax.axis_size("slab") - 1 - hop
    done_ref[...] = jnp.zeros_like(done_ref)

    def copy(ref, which, n):
        span = pl.ds(n * size, size)
        return pltpu.make_async_copy(
            held.at[:, span], ref.at[0, pl.ds(row0, rows), span], sems.at[which, n]
        )

    def emit(at, value):
        held[:, at : at + value.shape[1]] = value
        n, part = divmod(at + value.shape[1], size)
        if part == 0:
            pl.when(goes_down)(copy(down_ref, 0, n - 1).start)
            pl.when(goes_up)(copy(up_ref, 1, n - 1).start)

    product_kernel(hop, parts, False, cols_ref, far_ref, near_ref, *ins, ext, emit=emit)
    for n in range(count):
        pl.when(goes_down)(copy(down_ref, 0, n).wait)
        pl.when(goes_up)(copy(up_ref, 1, n).wait)


def product_kernel(hop, parts, split, cols_ref, far_ref, near_ref, *rest, emit=None):
    ins, (green_ref, total_ref), outs, ext = (
        rest[:parts],
        rest[parts : parts + 2],
        rest[parts + 2 : -1],
        rest[-1],
    )
    width = total_ref.shape[1]
    halo = far_ref.shape[1]
    bsize = green_ref.shape[-1]
    per_dev = width // bsize
    kcount = green_ref.shape[0] // per_dev
    slab = lax.axis_index("slab")
    active = jnp.logical_or(slab == hop, slab == lax.axis_size("slab") - 1 - hop)

    @pl.when(active)
    def _():
        left, right = edge_places(halo)
        ext[:, pl.ds(halo, halo)] = ins[0][:, pl.ds(left, halo)]
        ext[:, pl.ds(width, halo)] = ins[0][:, pl.ds(right, halo)]
        if parts == 2:
            ext[:, 2 * halo : width] = ins[1][...]
        elif width > 2 * halo:
            ext[:, 2 * halo : width] = ins[0][:, 2 * halo :]

        @pl.when(is_even())
        def _():
            ext[:, :halo] = far_ref[...]
            ext[:, halo + width :] = near_ref[...]

        @pl.when(jnp.logical_not(is_even()))
        def _():
            ext[:, :halo] = near_ref[...]
            ext[:, halo + width :] = far_ref[...]

        for i in range(per_dev):
            picked, blocks = [], []
            for k in range(kcount):
                at = pl.multiple_of(cols_ref[0, i * kcount + k] * bsize, bsize)
                picked.append(ext[:, pl.ds(at, bsize)])
                blocks.append(green_ref[i * kcount + k])
            value = lax.dot_general(
                jnp.concatenate(picked, 1),
                jnp.concatenate(blocks, 1),
                (((1,), (1,)), ((), ())),
                preferred_element_type=jnp.float32,
            )
            value = (value + total_ref[:, i * bsize : (i + 1) * bsize]).astype(jnp.bfloat16)
            at = i * bsize
            if emit:
                emit(at, value)
            elif at < halo:
                outs[0][:, pl.ds(pl.multiple_of(left + at, bsize), bsize)] = value
            elif at >= width - halo:
                at = at - (width - halo)
                outs[0][:, pl.ds(pl.multiple_of(right + at, bsize), bsize)] = value
            elif split:
                outs[1][:, at - halo : at - halo + bsize] = value
            else:
                outs[0][:, at + halo : at + halo + bsize] = value


def store_kernel(halo, hops, pieces, splits, given, *rest):
    ins, (down_ref, up_ref, done_ref, sems) = list(rest[: -4 - given]), rest[-4:]
    done_ref[...] = jnp.zeros_like(done_ref)
    width = down_ref.shape[2]
    slab = lax.axis_index("slab")
    last = lax.axis_size("slab") - 1
    traces = {}
    splits = list(splits)
    for h in hops:
        for j in range(len(pieces)):
            traces[h, j] = [ins.pop(0) for _ in range(1 + splits.pop(0))]

    def copies(h, out_ref, which):
        left, right = edge_places(halo)
        made = []
        for j, (row0, rows) in enumerate(pieces):
            edge, *mid = traces[h, j]
            moves = [
                (edge.at[:, pl.ds(left, halo)], 0, halo),
                (edge.at[:, pl.ds(right, halo)], width - halo, halo),
            ]
            size = width - 2 * halo
            if mid:
                moves.append((mid[0], halo, size))
            elif size:
                moves.append((edge.at[:, pl.ds(2 * halo, size)], halo, size))
            for src, col, size in moves:
                dst = out_ref.at[0, pl.ds(row0, rows), pl.ds(col, size)]
                made.append(pltpu.make_async_copy(src, dst, sems.at[which, len(made)]))
        return made

    plan = []
    for h in hops:
        plan.append((h, down_ref, 0, slab == h))
        plan.append((h, up_ref, 1, slab == last - h))
    for h, ref, which, chosen in plan:

        @pl.when(chosen)
        def _():
            for copy in copies(h, ref, which):
                copy.start()

    for h, ref, which, chosen in plan:

        @pl.when(chosen)
        def _():
            for copy in copies(h, ref, which):
                copy.wait()


def shards(thickness, layer_sources, green_down, column_down, green_up, column_up):
    slabs = lax.axis_size("slab")
    cross = lax.axis_size("cross")
    lateral = lax.axis_index("cross")
    depth, sources, width = layer_sources.shape
    bsize = green_down.shape[-1]
    per_dev = width // bsize
    total_blocks = per_dev * cross
    nblocks = green_down.shape[1]
    halo = HB * bsize
    chunks = chunk_rows(sources)

    layers = pinned(layer_sources, pltpu.HBM)
    greens = (pinned(green_down, pltpu.HBM), pinned(green_up, pltpu.HBM))

    def splits(h, j):
        return int(per_dev > 2 * HB and SPLIT[min(h * 3 // (slabs - 1), 2)][min(j, 1)])

    token = []

    def launch(kernel, ins, in_specs, out_shape, out_specs, scratch, mib, name, aliases=None):
        count = len(ins)
        ins, in_specs = [*ins, *token], [*in_specs, *[ANY] * len(token)]
        given = len(ins)

        def body(*refs):
            kernel(*refs[:count], *refs[given:])

        out = pl.pallas_call(
            body,
            out_shape=out_shape,
            in_specs=in_specs,
            out_specs=out_specs,
            scratch_shapes=scratch,
            input_output_aliases=aliases or {},
            compiler_params=params(mib),
            name=name,
        )(*ins)
        token[:] = [out[0 if name == "source" else -1]]
        return out

    def trace(rows, split):
        widths = [2 * halo, width - 2 * halo] if split else [width]
        return [pltpu.VMEM((rows, w), jnp.bfloat16) for w in widths]

    def local(low):
        cols = jnp.where(in_low_half() == low, column_down, column_up)
        return (cols - lateral * per_dev + HB) % total_blocks

    def fetch(hops):
        (block,) = launch(
            functools.partial(fetch_kernel, hops, hops[0] < slabs // 2),
            greens,
            [HBM, HBM],
            [pltpu.VMEM(green_down.shape[1:], jnp.bfloat16)],
            [VMEM],
            [pltpu.SemaphoreType.DMA],
            8,
            "fetch",
        )
        return block

    def source(j, row0, rows):
        out_shape = [pltpu.VMEM((rows, width), jnp.float32), *trace(rows, splits(0, j))]
        total, *out = launch(
            functools.partial(source_kernel, row0, halo),
            [thickness, layers],
            [SMEM, HBM],
            out_shape,
            [VMEM] * len(out_shape),
            [pltpu.VMEM((depth, rows, width), jnp.bfloat16), pltpu.SemaphoreType.DMA((depth,))],
            8,
            "source",
        )
        return total, *out

    def product(h, j, cols, far, near, got, green, total):
        rows = total.shape[0]
        ins = [pinned(x, pltpu.VMEM) for x in (far, near, *got, green, total)]
        out_shape = trace(rows, splits(h, j))
        return launch(
            functools.partial(product_kernel, h, len(got), len(out_shape) == 2),
            [cols, *ins],
            [SMEM] + [VMEM] * len(ins),
            out_shape,
            [VMEM] * len(out_shape),
            [pltpu.VMEM((rows, width + 2 * halo), jnp.bfloat16)],
            8,
            "product",
        )

    def last_product(j, cols, far, near, got, green, total, into):
        rows = total.shape[0]
        ins = [pinned(x, pltpu.VMEM) for x in (far, near, *got, green, total)]
        pieces = 4 if per_dev % 4 == 0 else 1
        return launch(
            functools.partial(last_product_kernel, slabs - 1, len(got), chunks[j][0]),
            [cols, *ins, *[pinned(x, pltpu.HBM) for x in into]],
            [SMEM] + [VMEM] * len(ins) + [HBM] * 2,
            [pltpu.HBM((1, sources, width), jnp.bfloat16)] * 2
            + [pltpu.VMEM((8, 128), jnp.float32)],
            [HBM, HBM, VMEM],
            [
                pltpu.VMEM((rows, width + 2 * halo), jnp.bfloat16),
                pltpu.VMEM((rows, width), jnp.bfloat16),
                pltpu.SemaphoreType.DMA((2, pieces)),
            ],
            8,
            "product",
            {len(ins) + 1: 0, len(ins) + 2: 1},
        )[:2]

    def store(hops, j0, pieces, arrays, into=()):
        ins = [pinned(x, pltpu.VMEM) for x in arrays]
        given = [pinned(x, pltpu.HBM) for x in into]
        *outs, _ = launch(
            functools.partial(
                store_kernel,
                halo,
                hops,
                pieces,
                [splits(h, j0 + j) for h in hops for j in range(len(pieces))],
                len(given),
            ),
            [*ins, *given],
            [VMEM] * len(ins) + [HBM] * len(given),
            [pltpu.HBM((1, sources, width), jnp.bfloat16)] * 2
            + [pltpu.VMEM((8, 128), jnp.float32)],
            [HBM, HBM, VMEM],
            [pltpu.SemaphoreType.DMA((2, len(pieces) * 3))],
            4,
            "store",
            {len(ins) + i: i for i in range(len(given))},
        )
        return outs

    def mate(c):
        return c ^ 1

    def next_chip(c):
        return (c + 1) % cross if c % 2 else (c - 1) % cross

    def hop(x, h):
        there = {s: s for s in range(slabs)}
        for a, b in ((h - 1, h), (slabs - h, slabs - 1 - h)):
            there[a], there[b] = b, a
        route = []
        for s in range(slabs):
            for c in range(cross):
                to = c if there[s] != s else mate(c)
                route.append((s * cross + c, there[s] * cross + to))
        return lax.ppermute(x, ("slab", "cross"), route)

    def to_mate(x):
        return lax.ppermute(x, "cross", [(c, mate(c)) for c in range(cross)])

    def to_next_chip(x, h):
        route = []
        for s in range(slabs):
            for c in range(cross):
                to = next_chip(c) if s in (h, slabs - 1 - h) else mate(c)
                route.append((s * cross + c, s * cross + to))
        return lax.ppermute(x, ("slab", "cross"), route)

    totals, made, moved = [], {}, {}
    for j, (row0, rows) in enumerate(chunks):
        total, *out = source(j, row0, rows)
        totals.append(total)
        made[0, j] = out
    cols = {low: local(low) for low in (True, False)}
    green = {}
    order = sorted(
        ((h, j) for h in range(1, slabs) for j in range(len(chunks))),
        key=lambda hj: (hj[0] + hj[1], hj[0]),
    )
    early = list(range(slabs - 1))
    groups = [list(range(1, slabs // 2)), list(range(slabs // 2, slabs - 1)), [slabs - 1]]
    groups = [g for g in groups if g]
    group_of = {h: g for g in range(len(groups)) for h in groups[g]}
    early = list(range(slabs - 1))
    outs, sides = [], {}

    def lateral(h, j):
        if (h, j) not in sides:
            edges = moved[h, j][0][:, : 2 * halo]
            if h == slabs - 1 and j:
                edges, _ = lax.optimization_barrier((edges, sides[h, j - 1][0]))
            sides[h, j] = (to_next_chip(edges[:, :halo], h), to_mate(edges[:, halo:]))
        return sides[h, j]

    def send(h, j):
        moved[h, j] = [hop(x, h) for x in made[h - 1, j]]

    for j in range(len(chunks)):
        send(1, j)
    for h, j in order:
        far, near = lateral(h, j)
        g = group_of[h]
        for ahead in range(g + 1 + (g + 1 < min(2, len(groups)))):
            if ahead not in green:
                green[ahead] = fetch(groups[ahead])
        if h == slabs - 1 and j == 0:
            arrays = [x for a in early for b in range(len(chunks)) for x in made[a, b]]
            outs = store(early, 0, chunks, arrays)
        given = (cols[h < slabs // 2], far, near, moved[h, j], green[g], totals[j])
        if h == slabs - 1:
            outs = last_product(j, *given, outs)
        else:
            made[h, j] = product(h, j, *given)
            send(h + 1, j)
        if (h, j) == (slabs - 2, 0) and len(groups) - 1 not in green:
            green[len(groups) - 1] = fetch(groups[-1])
    return tuple(outs)


def solution(mesh):
    return jax.shard_map(
        shards,
        mesh=mesh,
        in_specs=(
            P("slab"),
            P("slab", None, "cross"),
            P("slab", "cross", None, None),
            P("slab", "cross"),
            P("slab", "cross", None, None),
            P("slab", "cross"),
        ),
        out_specs=(P("slab", None, "cross"), P("slab", None, "cross")),
        check_vma=False,
    )
```
